512 devices in a mesh: tm: 32 (over x_lo, z), space: 16 (over y, x_hi, core).
Axes of the slice: x: 4 (x_hi: 2, x_lo: 2; x = x_hi * 2 + x_lo), y: 4, z: 16, core: 2. Of those that a mesh axis runs over, the one named last changes fastest.
Arguments:
- features: bfloat16 [64, 128, 80, 128], P('tm', 'space'), may hold values from -6 to 6
- norm_gain: float32 [128], replicated, may hold values from 0.1 to 1.9
- kernel: bfloat16 [3456, 256], P('space'), may hold values from -0.109375 to 0.109375
- cotangent: bfloat16 [64, 128, 80, 256], P('tm', 'space'), may hold values from -6 to 6
Outputs:
- decoded: bfloat16 [64, 128, 80, 256], P('tm', 'space')
- kernel_grad: float32 [3456, 256], P('space')
- input_grad: bfloat16 [64, 128, 80, 128], P('tm', 'space')
The draws below stay inside these ranges and needn't reach their ends.
All inputs are finite; a program needn't handle non-finite values.
Results may differ from the reference program's by a relative error of at most 0.005.
Values may be sent and summed in bfloat16 or wider, within the bound.
No kernel may reach another device: no remote copies, remote signals or barrier semaphores. Data moves between devices by JAX's collectives and lax.ppermute only.
A program may use at most 128 MiB of HBM per device.

```python
import jax
import jax.numpy as jnp
from jax import lax

CIN = 128
COUT = 256
COLS = 80
FRAMES = 64
HEIGHT = 128


def raised(array, own_key, source, target, shards_of, factor):
    owner, partner = [(jnp.arange(array.shape[position]) // (array.shape[position] // shards_of)).reshape([-1 if axis == position else 1 for axis in range(array.ndim)]) for position in (source, target)]
    chosen = jax.random.permutation(own_key, shards_of)[partner]
    strong = (owner == chosen) | (owner == (partner + shards_of // 2) % shards_of)
    return jnp.where(strong, factor * array, array)


def level_of(rng, extent, split, low, largest):
    level, own = 1.0, jax.random.fold_in(rng, 6)
    for dim, shards_of in split:
        draws = jnp.exp(jax.random.uniform(jax.random.fold_in(own, dim), (shards_of,), jnp.float32, low / len(split), largest / len(split)))
        level = level * jnp.repeat(draws, extent[dim] // shards_of).reshape([-1 if axis == dim else 1 for axis in range(len(extent))])
    return level


def noise(rng, dims, deviation, most, split=(), kind=jnp.bfloat16):
    drawn = jax.random.normal(rng, dims, jnp.float32) * deviation
    if len(split) > 0:
        drawn = level_of(rng, dims, split, -0.22, 0.18) * drawn
    return jnp.clip(drawn, min=-most, max=most).astype(kind)


def gaussian_with(stream_key, extent, spread, most, shards, heavy, kind=jnp.bfloat16):
    result = spread * jax.random.normal(stream_key, extent, jnp.float32)
    if shards:
        result = result * level_of(stream_key, extent, shards, -0.22, 0.18)
    return jnp.clip(raised(result, jax.random.fold_in(stream_key, 3), *heavy), -most, most).astype(kind)


def setup_inputs(seed: int = 0) -> dict:
    splits = jax.random.split(jax.random.key(seed), 5)
    return {
        "features": gaussian_with(splits[0], (FRAMES, HEIGHT, COLS, CIN), 1.0, 6.0, ((0, 32), (1, 16)), (1, 3, 16, 2.0)),
        "norm_gain": jnp.clip(1.0 + 0.18 * jax.random.normal(splits[1], (CIN,), jnp.float32), 0.1, 1.9),
        "kernel": noise(splits[2], (CIN * 27, COUT), (27 * CIN) ** -0.5, 0.109375, ((0, 16),)),
        "cotangent": noise(splits[3], (FRAMES, HEIGHT, COLS, COUT), 1.0, 6.0, ((0, 32), (1, 16))),
    }


epsilon = 1e-06

def activate(values, norm_gain):
    mean_square = lax.optimization_barrier(jnp.mean(values * values, axis=-1, keepdims=True))
    return jax.nn.silu(values * lax.rsqrt(mean_square + epsilon) * norm_gain)

def stack_taps(window, frames, rows, cols, flipped):
    pieces = []
    for frame_tap in range(3):
        for row_tap in range(3):
            for col_tap in range(3):
                first = 2 - frame_tap if flipped else frame_tap
                top = 2 - row_tap if flipped else row_tap
                left = 2 - col_tap if flipped else col_tap
                pieces.append(window[first:first + frames, top:top + rows, left:left + cols, :])
    return jnp.stack(pieces, axis=-1).reshape(frames * rows * cols, -1)

def reference(features, norm_gain, kernel, cotangent):
    frame_count, rows, cols = (features.shape[0], features.shape[1], features.shape[2])
    values = features.astype(jnp.float32)
    activated = activate(values, norm_gain).astype(jnp.bfloat16)
    act_pad = jnp.pad(activated, ((2, 0), (1, 1), (1, 1), (0, 0)))
    grad_pad = jnp.pad(cotangent, ((0, 2), (1, 1), (1, 1), (0, 0)))
    transposed = kernel.reshape(CIN, 27, COUT).transpose(2, 1, 0).reshape(COUT * 27, CIN)

    def one_frame(total, frame):
        window = lax.dynamic_slice_in_dim(act_pad, frame, 3, 0)
        patches = stack_taps(window, 1, rows, cols, False)
        out_frame = jnp.dot(patches, kernel, preferred_element_type=jnp.float32).astype(jnp.bfloat16)
        grad_window = lax.dynamic_slice_in_dim(grad_pad, frame, 3, 0)
        grad_patches = stack_taps(grad_window, 1, rows, cols, True)
        act_grad = jnp.dot(grad_patches, transposed, preferred_element_type=jnp.float32)
        grad_rows = lax.dynamic_slice_in_dim(cotangent, frame, 1, 0).reshape(rows * cols, COUT)
        total = total + lax.dot_general(patches, grad_rows, (((0,), (0,)), ((), ())), preferred_element_type=jnp.float32)
        return (total, (out_frame, act_grad))
    start = jnp.zeros((CIN * 27, COUT), jnp.float32)
    kernel_grad, (decoded, act_grad) = lax.scan(one_frame, start, jnp.arange(frame_count, dtype=jnp.int32))
    decoded = decoded.reshape(frame_count, rows, cols, COUT)
    act_grad = act_grad.reshape(frame_count, rows, cols, CIN)
    _, pull = jax.vjp(lambda inner: activate(inner, norm_gain), values)
    input_grad = pull(act_grad)[0].astype(jnp.bfloat16)
    return (decoded, kernel_grad, input_grad)
```

```python
import jax
import jax.numpy as jnp
from jax import lax
from jax.experimental import pallas as pl
from jax.experimental.pallas import tpu as pltpu
from jax.sharding import Mesh, PartitionSpec as P

epsilon = 1e-06
F32 = jnp.float32
BF16 = jnp.bfloat16
TM = ("xl", "z1", "z0")
SPACE = ("y", "xh", "co")
SIZES = (2, 4, 4, 4, 2, 2)
AXES = TM + SPACE
TMS, SPACES = 32, 16


def shift(block, target):
    route = []
    for t in range(TMS):
        for s in range(SPACES):
            u, v = target(t, s)
            if 0 <= u < TMS and 0 <= v < SPACES:
                route.append((t * SPACES + s, u * SPACES + v))
    return lax.ppermute(block, AXES, route)


def beside(block):
    cols = block.shape[1]
    col = lax.broadcasted_iota(jnp.int32, block.shape, 1)
    left = jnp.where(col == 0, 0.0, pltpu.roll(block, 1, 1))
    right = jnp.where(col == cols - 1, 0.0, pltpu.roll(block, cols - 1, 1))
    return jnp.concatenate([left, block, right], axis=-1).astype(BF16)


def activated(block, gain):
    frames, rows, cols, channels = block.shape
    v = block.reshape(frames * rows, cols, channels).astype(F32)
    z = v * lax.rsqrt(jnp.mean(v * v, axis=-1, keepdims=True) + epsilon) * gain
    return z / (1.0 + jnp.exp(-z))


def gradient(act, pad):
    frames = act.shape[0]
    rows = act.reshape(frames * 640, 384)
    shifted = [pad[:, 2 - b : 10 - b].reshape(frames * 640, 256) for b in range(3)]
    return lax.dot_general(
        rows,
        jnp.concatenate(shifted, axis=-1),
        (((0,), (0,)), ((), ())),
        preferred_element_type=F32,
    )


def prepare_body(own, gain, cot, act, held):
    g = gain[...].reshape(1, 1, 128)
    act[...] = beside(activated(own[...], g)).reshape(2, 8, 80, 384)
    held[...] = cot[...]


def own_grad_body(act, cot, top, low, pad, edges, part):
    pad[:, 1:9] = cot[...]
    edges[:, 0:1] = top[...]
    edges[:, 1:2] = low[...]
    pad[:, 0:1] = top[...]
    pad[:, 9:10] = low[...]
    part[0] = gradient(act[0:1], pad[1:2])
    part[1] = gradient(act[...], pad[...])


def rest_grad_body(
    core, prev, gain, own_act, pad, part, act, first, last, keep, send, total
):
    g = gain[...].reshape(1, 1, 128)
    a32 = activated(prev[...], g)
    act[...] = beside(a32).reshape(2, 8, 80, 384)
    first[0:2] = act[:, 0:1, :, 128:256]
    last[0:2] = act[:, 7:8, :, 128:256]
    first[2:4] = own_act[:, 0:1, :, 128:256]
    last[2:4] = own_act[:, 7:8, :, 128:256]
    total[0] = gradient(act[...], pad[...])
    total[1] = part[0] + gradient(act[1:2], pad[0:1])

    def tap(index):
        a, b, e = index // 9, index // 3 % 3, index % 3
        ref = part.at[1] if a == 2 else total.at[a]
        return ref, 128 * e, 256 * b

    def pack(even, odd):
        for pair in range(14):
            for chip in range(8):
                for out, parity in ((even, 0), (odd, 1)):
                    blocks = []
                    for index in (2 * pair, min(2 * pair + 1, 26)):
                        ref, row, col = tap(index)
                        row = row + 16 * chip + 8 * parity
                        blocks.append(ref[row : row + 8, col : col + 256])
                    if pair == 13:
                        blocks[1] = jnp.zeros_like(blocks[1])
                    both = jnp.concatenate(blocks, axis=0).astype(BF16)
                    out[chip, 16 * pair : 16 * pair + 16] = both

    @pl.when(core[0] == 0)
    def _():
        pack(keep, send)

    @pl.when(core[0] != 0)
    def _():
        pack(send, keep)


VMEM = pl.BlockSpec(memory_space=pltpu.VMEM)
SMEM = pl.BlockSpec(memory_space=pltpu.SMEM)


def prepare(own, gain, cot):
    return pl.pallas_call(
        prepare_body,
        out_shape=(
            jax.ShapeDtypeStruct((2, 8, 80, 384), BF16),
            jax.ShapeDtypeStruct((2, 8, 80, 256), BF16),
        ),
        in_specs=[VMEM] * 3,
        out_specs=(VMEM,) * 2,
        compiler_params=pltpu.CompilerParams(vmem_limit_bytes=8 << 20),
        name="prepare",
    )(own, gain, cot)


def own_grad(act, cot, top, low):
    return pl.pallas_call(
        own_grad_body,
        out_shape=(
            jax.ShapeDtypeStruct((2, 10, 80, 256), BF16),
            jax.ShapeDtypeStruct((2, 2, 80, 256), BF16),
            jax.ShapeDtypeStruct((2, 384, 768), F32),
        ),
        in_specs=[VMEM] * 4,
        out_specs=(VMEM,) * 3,
        compiler_params=pltpu.CompilerParams(vmem_limit_bytes=10 << 20),
        cost_estimate=pl.CostEstimate(
            flops=1280 * 3456 * 256, bytes_accessed=6 << 20, transcendentals=0
        ),
        name="own_grad",
    )(act, cot, top, low)


def rest_grad(core, prev, gain, own_act, pad, part):
    return pl.pallas_call(
        rest_grad_body,
        out_shape=(
            jax.ShapeDtypeStruct((2, 8, 80, 384), BF16),
            jax.ShapeDtypeStruct((4, 1, 80, 128), BF16),
            jax.ShapeDtypeStruct((4, 1, 80, 128), BF16),
            jax.ShapeDtypeStruct((8, 224, 256), BF16),
            jax.ShapeDtypeStruct((8, 224, 256), BF16),
        ),
        in_specs=[SMEM] + [VMEM] * 5,
        out_specs=(VMEM,) * 5,
        scratch_shapes=[pltpu.VMEM((2, 384, 768), F32)],
        compiler_params=pltpu.CompilerParams(vmem_limit_bytes=12 << 20),
        cost_estimate=pl.CostEstimate(
            flops=1280 * 3456 * 256, bytes_accessed=6 << 20, transcendentals=1 << 18
        ),
        name="rest_grad",
    )(core, prev, gain, own_act, pad, part)


def call(body, name, out_shape, args, specs=None, scratch=()):
    return pl.pallas_call(
        body,
        out_shape=out_shape,
        in_specs=specs or [VMEM] * len(args),
        out_specs=VMEM,
        scratch_shapes=scratch,
        compiler_params=pltpu.CompilerParams(vmem_limit_bytes=6 << 20),
        name=name,
    )(*args)


def add_cores(keep, got):
    def body(keep_ref, got_ref, out_ref):
        out_ref[...] = (keep_ref[...].astype(F32) + got_ref[...].astype(F32)).astype(BF16)

    shape = jax.ShapeDtypeStruct(keep.shape, BF16)
    return call(body, "add_cores", shape, (keep, got))


def add_chips(rows):
    def body(rows_ref, out_ref):
        total = rows_ref[0].astype(F32)
        for chip in range(1, 8):
            total = total + rows_ref[chip].astype(F32)
        for side in range(2):
            for quarter in range(4):
                block = total[56 * quarter : 56 * quarter + 56, 128 * side : 128 * side + 128]
                out_ref[4 * side + quarter] = block

    shape = jax.ShapeDtypeStruct((8, 56, 128), F32)
    return call(body, "add_chips", shape, (rows,))


def add_parts(parts):
    def body(parts_ref, out_ref):
        out_ref[...] = jnp.sum(parts_ref[...], axis=0)

    return call(body, "add_parts", jax.ShapeDtypeStruct(parts.shape[1:], F32), (parts,))


def add_far(own, near, far, farthest):
    def body(own_ref, near_ref, far_ref, farthest_ref, out_ref):
        total = (own_ref[...] + near_ref[...]) + (far_ref[...] + farthest_ref[...])
        out_ref[...] = jnp.broadcast_to(total, (8, 56, 128))

    shape = jax.ShapeDtypeStruct((8, 56, 128), F32)
    return call(body, "add_far", shape, (own, near, far, farthest))


def finish(whole):
    def body(whole_ref, out_ref, side_ref):
        for side in range(2):
            for tap in range(27):
                row = 8 * tap
                block = whole_ref[4 * side + row // 56, row % 56 : row % 56 + 8]
                side_ref[side, pl.ds(tap, 8, stride=27), :] = block
            out_ref[:, 128 * side : 128 * side + 128] = side_ref[side]

    shape = jax.ShapeDtypeStruct((216, 256), F32)
    scratch = (pltpu.VMEM((2, 216, 128), F32),)
    return call(body, "finish", shape, (whole,), None, scratch)


def outputs_body(
    pieces,
    prev_act,
    own_act,
    top,
    low,
    own,
    pad,
    next_cot,
    next_edges,
    gain,
    dec,
    ing,
    kern,
    raw,
    edge,
):
    for chip in range(8):
        for side in range(2):
            columns = slice(128 * side, 128 * side + 128)
            for half in range(2):
                raw[side, half] = pieces[2 * chip + half, :, columns].astype(F32)
            for tap in range(27):
                rows = [raw[side, half, pl.ds(tap, 8, stride=27), :] for half in range(2)]
                rows = jnp.concatenate(rows, axis=0).astype(BF16)
                kern[tap, 16 * chip : 16 * chip + 16, columns] = rows
    edge[0] = beside(top[...].reshape(4, 80, 128).astype(F32))
    edge[1] = beside(low[...].reshape(4, 80, 128).astype(F32))

    def act_rows(frame, at):
        act, index = (prev_act, frame) if frame < 2 else (own_act, frame - 2)
        if at < 0:
            rows = jnp.concatenate([edge[0, frame : frame + 1], act[index, 0:3]], axis=0)
        elif at > 4:
            rows = jnp.concatenate([act[index, 5:8], edge[1, frame : frame + 1]], axis=0)
        else:
            rows = act[index, at : at + 4]
        return rows.reshape(320, 384)

    for t in range(2):
        for half in range(2):
            patches = [
                act_rows(t + a, 4 * half + b - 1) for a in range(3) for b in range(3)
            ]
            out = jnp.dot(
                jnp.concatenate(patches, axis=-1),
                kern[...].reshape(3456, 256),
                preferred_element_type=F32,
            )
            dec[t, 4 * half : 4 * half + 4] = out.astype(BF16).reshape(4, 80, 256)

    def cot_rows(frame, at):
        if frame < 2:
            return pad[frame, at + 1 : at + 5].reshape(320, 256)
        cot, edges = next_cot[frame - 2], next_edges[frame - 2]
        if at < 0:
            rows = jnp.concatenate([edges[0:1], cot[0:3]], axis=0)
        elif at > 4:
            rows = jnp.concatenate([cot[5:8], edges[1:2]], axis=0)
        else:
            rows = cot[at : at + 4]
        return rows.reshape(320, 256)

    g = gain[...].reshape(1, 1, 128)
    for s in range(2):
        for half in range(2):
            sums = jnp.zeros((320, 384), F32)
            for a in range(3):
                for b in range(3):
                    window = cot_rows(s + 2 - a, 4 * half + 1 - b)
                    weights = kern[9 * a + 3 * b : 9 * a + 3 * b + 3].reshape(384, 256)
                    sums = sums + lax.dot_general(
                        window, weights, (((1,), (1,)), ((), ())), preferred_element_type=F32
                    )
            sums = sums.reshape(4, 80, 384)
            left, mid, right = sums[..., :128], sums[..., 128:256], sums[..., 256:]
            col = lax.broadcasted_iota(jnp.int32, mid.shape, 1)
            grad = mid + jnp.where(col == 79, 0.0, pltpu.roll(left, 79, 1))
            grad = grad + jnp.where(col == 0, 0.0, pltpu.roll(right, 1, 1))
            v = own[s, 4 * half : 4 * half + 4].astype(F32)
            scale = lax.rsqrt(jnp.mean(v * v, axis=-1, keepdims=True) + epsilon)
            normed = v * scale
            z = normed * g
            gate = 1.0 / (1.0 + jnp.exp(-z))
            dn = grad * (gate * (1.0 + z * (1.0 - gate))) * g
            out = scale * (dn - normed * jnp.mean(dn * normed, axis=-1, keepdims=True))
            ing[s, 4 * half : 4 * half + 4] = out.astype(BF16)


def outputs(pieces, prev_act, own_act, top, low, own, pad, next_cot, next_edges, gain):
    return pl.pallas_call(
        outputs_body,
        out_shape=(
            jax.ShapeDtypeStruct((2, 8, 80, 256), BF16),
            jax.ShapeDtypeStruct((2, 8, 80, 128), BF16),
        ),
        in_specs=[VMEM] * 10,
        out_specs=(VMEM,) * 2,
        scratch_shapes=[
            pltpu.VMEM((27, 128, 256), BF16),
            pltpu.VMEM((2, 2, 216, 128), F32),
            pltpu.VMEM((2, 4, 80, 384), BF16),
        ],
        compiler_params=pltpu.CompilerParams(vmem_limit_bytes=20 << 20),
        cost_estimate=pl.CostEstimate(
            flops=4 * 1280 * 3456 * 256, bytes_accessed=8 << 20, transcendentals=1 << 18
        ),
        name="outputs",
    )(pieces, prev_act, own_act, top, low, own, pad, next_cot, next_edges, gain)


def on_device(features, norm_gain, kernel, cotangent):
    core = lax.axis_index("co").reshape(1)
    prev = shift(features, lambda t, s: (t + 1, s))
    top = shift(cotangent[:, 7:], lambda t, s: (t, s + 1))
    low = shift(cotangent[:, :1], lambda t, s: (t, s - 1))
    pieces = lax.all_gather(kernel, SPACE, axis=0)
    next_cot = shift(cotangent, lambda t, s: (t - 1, s))
    own_act, held = prepare(features, norm_gain, cotangent)
    pad, edges, part = own_grad(own_act, held, top, low)
    prev, next_cot = lax.optimization_barrier((prev, next_cot))
    prev_act, first, last, keep, send = rest_grad(core, prev, norm_gain, own_act, pad, part)
    next_edges = shift(edges, lambda t, s: (t - 1, s))
    act_top = shift(last, lambda t, s: (t, s + 1))
    act_low = shift(first, lambda t, s: (t, s - 1))
    both = add_cores(keep, shift(send, lambda t, s: (t, s ^ 1)))
    rows = lax.all_to_all(both, ("y", "xh"), 0, 0, tiled=True)
    rows, next_edges, act_top, act_low = lax.optimization_barrier(
        (rows, next_edges, act_top, act_low)
    )
    parts = add_chips(rows)
    part = add_parts(lax.all_to_all(parts, ("xl", "z0"), 0, 0, tiled=True))
    near, far, farthest = [shift(part, lambda t, s: (t ^ step, s)) for step in (4, 8, 12)]
    decoded, input_grad = outputs(
        pieces,
        prev_act,
        own_act,
        act_top,
        act_low,
        features,
        pad,
        next_cot,
        next_edges,
        norm_gain,
    )
    far, decoded, input_grad = lax.optimization_barrier((far, decoded, input_grad))
    whole = add_far(part, near, far, farthest)
    whole = lax.all_to_all(whole, ("xl", "z0"), 0, 0, tiled=True)
    kernel_grad = finish(whole)
    return (decoded, kernel_grad, input_grad)


def solution(mesh):
    fine = Mesh(mesh.devices.reshape(SIZES), AXES)
    split = P(TM, SPACE, None, None)
    rows = P(SPACE, None)
    return jax.shard_map(
        on_device,
        mesh=fine,
        in_specs=(split, P(), rows, split),
        out_specs=(split, rows, split),
        check_vma=False,
    )
```

```python
import jax
import jax.numpy as jnp
from jax import lax
from jax.experimental import pallas as pl
from jax.experimental.pallas import tpu as pltpu
from jax.sharding import Mesh, PartitionSpec as P

epsilon = 1e-06
F32 = jnp.float32
BF16 = jnp.bfloat16
TM = ("xl", "z1", "z0")
SPACE = ("y", "xh", "co")
SIZES = (2, 4, 4, 4, 2, 2)
AXES = TM + SPACE
TMS, SPACES = 32, 16


def shift(block, target):
    route = []
    for t in range(TMS):
        for s in range(SPACES):
            u, v = target(t, s)
            if 0 <= u < TMS and 0 <= v < SPACES:
                route.append((t * SPACES + s, u * SPACES + v))
    return lax.ppermute(block, AXES, route)


def beside(block):
    cols = block.shape[1]
    col = lax.broadcasted_iota(jnp.int32, block.shape, 1)
    left = jnp.where(col == 0, 0.0, pltpu.roll(block, 1, 1))
    right = jnp.where(col == cols - 1, 0.0, pltpu.roll(block, cols - 1, 1))
    return jnp.concatenate([left, block, right], axis=-1).astype(BF16)


def activated(block, gain):
    frames, rows, cols, channels = block.shape
    v = block.reshape(frames * rows, cols, channels).astype(F32)
    z = v * lax.rsqrt(jnp.mean(v * v, axis=-1, keepdims=True) + epsilon) * gain
    return z / (1.0 + jnp.exp(-z))


def gradient(act, pad):
    frames = act.shape[0]
    rows = act.reshape(frames * 640, 384)
    shifted = [pad[:, 2 - b : 10 - b].reshape(frames * 640, 256) for b in range(3)]
    return lax.dot_general(
        rows,
        jnp.concatenate(shifted, axis=-1),
        (((0,), (0,)), ((), ())),
        preferred_element_type=F32,
    )


def kernel_grad_body(
    core, prev, own, gain, cot, top, low, cot_edges, row_edges, keep, send, act, pad, part, total
):
    g = gain[...].reshape(1, 1, 128)
    act[2:4] = beside(activated(own[...], g)).reshape(2, 8, 80, 384)
    act[0:2] = beside(activated(prev[...], g)).reshape(2, 8, 80, 384)
    for index, outer in enumerate((top, low)):
        row_edges[:, index : index + 1] = outer[:, :, :, :128]
        cot_edges[:, index : index + 1] = outer[:, :, :, 128:]
        pad[:, 9 * index : 9 * index + 1] = outer[:, :, :, 128:]
    pad[:, 1:9] = cot[...]
    for a in range(3):
        part_of = total.at[a] if a < 2 else part
        part_of[...] = gradient(act[a : a + 2], pad[...])

    def tap(index):
        a, b, e = index // 9, index // 3 % 3, index % 3
        ref = part if a == 2 else total.at[a]
        return ref, 128 * e, 256 * b

    def pack(even, odd):
        for pair in range(14):
            for chip in range(8):
                for out, parity in ((even, 0), (odd, 1)):
                    blocks = []
                    for index in (2 * pair, min(2 * pair + 1, 26)):
                        ref, row, col = tap(index)
                        row = row + 16 * chip + 8 * parity
                        blocks.append(ref[row : row + 8, col : col + 256])
                    if pair == 13:
                        blocks[1] = jnp.zeros_like(blocks[1])
                    both = jnp.concatenate(blocks, axis=0).astype(BF16)
                    out[chip, 16 * pair : 16 * pair + 16] = both

    @pl.when(core[0] == 0)
    def _():
        pack(keep, send)

    @pl.when(core[0] != 0)
    def _():
        pack(send, keep)


VMEM = pl.BlockSpec(memory_space=pltpu.VMEM)
SMEM = pl.BlockSpec(memory_space=pltpu.SMEM)
ANY = pl.BlockSpec(memory_space=pl.ANY)


def kernel_gradient(core, prev, own, gain, cot, top, low):
    return pl.pallas_call(
        kernel_grad_body,
        out_shape=(
            jax.ShapeDtypeStruct((2, 2, 80, 256), BF16),
            jax.ShapeDtypeStruct((2, 2, 80, 128), BF16),
            jax.ShapeDtypeStruct((8, 224, 256), BF16),
            jax.ShapeDtypeStruct((8, 224, 256), BF16),
        ),
        in_specs=[SMEM] + [VMEM] * 6,
        out_specs=(VMEM,) * 4,
        scratch_shapes=[
            pltpu.VMEM((4, 8, 80, 384), BF16),
            pltpu.VMEM((2, 10, 80, 256), BF16),
            pltpu.VMEM((384, 768), F32),
            pltpu.VMEM((2, 384, 768), F32),
        ],
        compiler_params=pltpu.CompilerParams(vmem_limit_bytes=20 << 20),
        cost_estimate=pl.CostEstimate(
            flops=2 * 1280 * 3456 * 256, bytes_accessed=6 << 20, transcendentals=1 << 18
        ),
        name="kernel_grad",
    )(core, prev, own, gain, cot, top, low)


def call(body, name, out_shape, args, specs=None, scratch=()):
    return pl.pallas_call(
        body,
        out_shape=out_shape,
        in_specs=specs or [VMEM] * len(args),
        out_specs=VMEM,
        scratch_shapes=scratch,
        compiler_params=pltpu.CompilerParams(vmem_limit_bytes=6 << 20),
        name=name,
    )(*args)


def add_cores(keep, got):
    def body(keep_ref, got_ref, out_ref):
        out_ref[...] = (keep_ref[...].astype(F32) + got_ref[...].astype(F32)).astype(BF16)

    shape = jax.ShapeDtypeStruct(keep.shape, BF16)
    return call(body, "add_cores", shape, (keep, got))


def add_chips(rows):
    def body(rows_ref, out_ref):
        total = rows_ref[0].astype(F32)
        for chip in range(1, 8):
            total = total + rows_ref[chip].astype(F32)
        for side in range(2):
            for quarter in range(4):
                block = total[56 * quarter : 56 * quarter + 56, 128 * side : 128 * side + 128]
                out_ref[4 * side + quarter] = block

    shape = jax.ShapeDtypeStruct((8, 56, 128), F32)
    return call(body, "add_chips", shape, (rows,))


def add_parts(parts, copies):
    shape = (copies, *parts.shape[1:])

    def body(parts_ref, out_ref):
        total = parts_ref[0]
        for index in range(1, parts.shape[0]):
            total = total + parts_ref[index]
        out_ref[...] = jnp.broadcast_to(total, shape)

    return call(body, "add_parts", jax.ShapeDtypeStruct(shape, F32), (parts,))


def repeat(rows, copies):
    shape = (copies, *rows.shape)

    def body(rows_ref, out_ref):
        for index in range(copies):
            out_ref[index] = rows_ref[...]

    return call(body, "repeat", jax.ShapeDtypeStruct(shape, rows.dtype), (rows,))


def finish(whole):
    def body(whole_ref, out_ref, side_ref):
        for side in range(2):
            for tap in range(27):
                row = 8 * tap
                block = whole_ref[4 * side + row // 56, row % 56 : row % 56 + 8]
                side_ref[side, pl.ds(tap, 8, stride=27), :] = block
            out_ref[:, 128 * side : 128 * side + 128] = side_ref[side]

    shape = jax.ShapeDtypeStruct((216, 256), F32)
    scratch = (pltpu.VMEM((2, 216, 128), F32),)
    return call(body, "finish", shape, (whole,), None, scratch)


def decode_body(
    core,
    mine_hbm,
    other_hbm,
    prev_hbm,
    own_hbm,
    gain,
    dec_hbm,
    kern_hbm,
    kern,
    raw,
    act,
    mine,
    other,
    prev,
    own,
    dec,
    sems,
):
    pairs = ((mine_hbm, mine), (other_hbm, other), (prev_hbm, prev), (own_hbm, own))
    loads = [
        pltpu.make_async_copy(source, held, sems.at[index])
        for index, (source, held) in enumerate(pairs)
    ]
    for load in loads:
        load.start()
    loads[0].wait()
    loads[1].wait()
    for chip in range(8):
        for side in range(2):
            columns = slice(128 * side, 128 * side + 128)
            one, two = [ref[chip, :, columns].astype(F32) for ref in (mine, other)]
            raw[side, 0] = jnp.where(core[0] == 0, one, two)
            raw[side, 1] = jnp.where(core[0] == 0, two, one)
            for tap in range(27):
                rows = [raw[side, half, pl.ds(tap, 8, stride=27), :] for half in range(2)]
                rows = jnp.concatenate(rows, axis=0).astype(BF16)
                kern[tap, 16 * chip : 16 * chip + 16, columns] = rows
    stores = [pltpu.make_async_copy(kern, kern_hbm, sems.at[4])]
    stores[0].start()
    loads[2].wait()
    loads[3].wait()
    g = gain[...].reshape(1, 1, 128)
    act[0:2] = beside(activated(prev[...], g)).reshape(2, 8, 80, 384)
    act[2:4] = beside(activated(own[...], g)).reshape(2, 8, 80, 384)
    for t in range(2):
        for half in range(2):
            at = 3 * half
            patches = [
                act[t + a, at + b : at + b + 3].reshape(240, 384)
                for a in range(3)
                for b in range(3)
            ]
            out = jnp.dot(
                jnp.concatenate(patches, axis=-1),
                kern[...].reshape(3456, 256),
                preferred_element_type=F32,
            )
            dec[t, at : at + 3] = out.astype(BF16).reshape(3, 80, 256)
            stores.append(
                pltpu.make_async_copy(
                    dec.at[t, at : at + 3],
                    dec_hbm.at[t, at + 1 : at + 4],
                    sems.at[5 + 2 * t + half],
                )
            )
            stores[-1].start()
    for store in stores:
        store.wait()


def decode(core, mine, other, prev, own, gain):
    return pl.pallas_call(
        decode_body,
        out_shape=(
            jax.ShapeDtypeStruct((2, 8, 80, 256), BF16),
            jax.ShapeDtypeStruct((27, 128, 256), BF16),
        ),
        in_specs=[SMEM] + [ANY] * 4 + [VMEM],
        out_specs=(ANY, ANY),
        scratch_shapes=[
            pltpu.VMEM((27, 128, 256), BF16),
            pltpu.VMEM((2, 2, 216, 128), F32),
            pltpu.VMEM((4, 8, 80, 384), BF16),
            pltpu.VMEM((8, 216, 256), BF16),
            pltpu.VMEM((8, 216, 256), BF16),
            pltpu.VMEM((2, 8, 80, 128), BF16),
            pltpu.VMEM((2, 8, 80, 128), BF16),
            pltpu.VMEM((2, 6, 80, 256), BF16),
            pltpu.SemaphoreType.DMA((9,)),
        ],
        compiler_params=pltpu.CompilerParams(vmem_limit_bytes=60 << 20),
        cost_estimate=pl.CostEstimate(
            flops=2 * 1280 * 3456 * 256, bytes_accessed=8 << 20, transcendentals=0
        ),
        name="decode",
    )(core, mine, other, prev, own, gain)


def finish_outputs_body(
    kern_hbm,
    prev_hbm,
    own_hbm,
    prev_edges,
    own_edges,
    cot_hbm,
    edges,
    next_cot_hbm,
    next_edges,
    gain,
    inner,
    dec,
    ing,
    act,
    rows_out,
    kern,
    prev,
    own,
    cot,
    next_cot,
    sems,
):
    pairs = (
        (own_hbm, own),
        (prev_hbm, prev),
        (kern_hbm, kern),
        (cot_hbm, cot),
        (next_cot_hbm, next_cot),
    )
    loads = [
        pltpu.make_async_copy(source, held, sems.at[4 + index])
        for index, (source, held) in enumerate(pairs)
    ]
    for load in loads:
        load.start()
    g = gain[...].reshape(1, 1, 128)
    loads[0].wait()
    loads[1].wait()
    for index, at in enumerate((0, 6)):
        first = 1 - index
        sources = ((prev, prev_edges), (own, own_edges))
        for frames, (block, outer) in enumerate(sources):
            at_frames = slice(2 * frames, 2 * frames + 2)
            act[at_frames, first : first + 2] = beside(
                activated(block[:, at : at + 2], g)
            ).reshape(2, 2, 80, 384)
            act[at_frames, 2 * index : 2 * index + 1] = beside(
                activated(outer[:, index : index + 1], g)
            ).reshape(2, 1, 80, 384)
        if index == 0:
            loads[2].wait()
        patches = [
            act[a : a + 2, b].reshape(160, 384) for a in range(3) for b in range(3)
        ]
        out = jnp.dot(
            jnp.concatenate(patches, axis=-1),
            kern[...].reshape(3456, 256),
            preferred_element_type=F32,
        )
        rows_out[index] = out.astype(BF16).reshape(2, 80, 256)
    copies = [
        pltpu.make_async_copy(
            rows_out.at[index, t], dec.at[t, 7 * index], sems.at[2 * index + t]
        )
        for index in range(2)
        for t in range(2)
    ]
    for copy in copies:
        copy.start()
    loads[3].wait()
    loads[4].wait()

    def cot_rows(frame, at):
        ref, outer, frame = (
            (cot, edges, frame) if frame < 2 else (next_cot, next_edges, frame - 2)
        )
        if at < 0:
            rows = jnp.concatenate([outer[frame, 0:1], ref[frame, 0:3]], axis=0)
        elif at > 4:
            rows = jnp.concatenate([ref[frame, 5:8], outer[frame, 1:2]], axis=0)
        else:
            rows = ref[frame, at : at + 4]
        return rows.reshape(320, 256)

    for s in range(2):
        for half in range(2):
            sums = jnp.zeros((320, 384), F32)
            for a in range(3):
                for b in range(3):
                    window = cot_rows(s + 2 - a, 4 * half + 1 - b)
                    weights = kern[9 * a + 3 * b : 9 * a + 3 * b + 3].reshape(384, 256)
                    sums = sums + lax.dot_general(
                        window, weights, (((1,), (1,)), ((), ())), preferred_element_type=F32
                    )
            sums = sums.reshape(4, 80, 384)
            left, mid, right = sums[..., :128], sums[..., 128:256], sums[..., 256:]
            col = lax.broadcasted_iota(jnp.int32, mid.shape, 1)
            grad = mid + jnp.where(col == 79, 0.0, pltpu.roll(left, 79, 1))
            grad = grad + jnp.where(col == 0, 0.0, pltpu.roll(right, 1, 1))
            v = own[s, 4 * half : 4 * half + 4].astype(F32)
            scale = lax.rsqrt(jnp.mean(v * v, axis=-1, keepdims=True) + epsilon)
            normed = v * scale
            z = normed * g
            gate = 1.0 / (1.0 + jnp.exp(-z))
            dn = grad * (gate * (1.0 + z * (1.0 - gate))) * g
            out = scale * (dn - normed * jnp.mean(dn * normed, axis=-1, keepdims=True))
            ing[s, 4 * half : 4 * half + 4] = out.astype(BF16)
    for copy in copies:
        copy.wait()


def finish_outputs(
    kern, prev, own, prev_edges, own_edges, cot, edges, next_cot, next_edges, gain, inner
):
    return pl.pallas_call(
        finish_outputs_body,
        out_shape=(
            jax.ShapeDtypeStruct((2, 8, 80, 256), BF16),
            jax.ShapeDtypeStruct((2, 8, 80, 128), BF16),
        ),
        in_specs=[ANY] * 3 + [VMEM] * 2 + [ANY, VMEM, ANY, VMEM, VMEM, ANY],
        out_specs=(ANY, VMEM),
        input_output_aliases={10: 0},
        scratch_shapes=[
            pltpu.VMEM((4, 3, 80, 384), BF16),
            pltpu.VMEM((2, 2, 80, 256), BF16),
            pltpu.VMEM((27, 128, 256), BF16),
            pltpu.VMEM((2, 8, 80, 128), BF16),
            pltpu.VMEM((2, 8, 80, 128), BF16),
            pltpu.VMEM((2, 8, 80, 256), BF16),
            pltpu.VMEM((2, 8, 80, 256), BF16),
            pltpu.SemaphoreType.DMA((9,)),
        ],
        compiler_params=pltpu.CompilerParams(vmem_limit_bytes=60 << 20),
        cost_estimate=pl.CostEstimate(
            flops=2 * 1280 * 3456 * 256, bytes_accessed=8 << 20, transcendentals=1 << 18
        ),
        name="finish_outputs",
    )(kern, prev, own, prev_edges, own_edges, cot, edges, next_cot, next_edges, gain, inner)


def on_device(features, norm_gain, kernel, cotangent):
    core = lax.axis_index("co").reshape(1)
    tie = lax.optimization_barrier
    next_cot = shift(cotangent, lambda t, s: (t - 1, s))
    prev = shift(features, lambda t, s: (t + 1, s))
    last = jnp.concatenate([features[:, 7:], cotangent[:, 7:]], axis=-1)
    first = jnp.concatenate([features[:, :1], cotangent[:, :1]], axis=-1)
    top = shift(last, lambda t, s: (t, s + 1))
    low = shift(first, lambda t, s: (t, s - 1))
    next_cot, prev, top, low, repeated = tie((next_cot, prev, top, low, repeat(kernel, 8)))
    mine = lax.all_to_all(repeated, ("y", "xh"), 0, 0, tiled=True)
    edges, own_edges, keep, send = kernel_gradient(
        core, prev, features, norm_gain, cotangent, top, low
    )
    next_edges = shift(edges, lambda t, s: (t - 1, s))
    prev_edges = shift(own_edges, lambda t, s: (t + 1, s))
    keep, mine = tie((keep, mine))
    other = shift(mine, lambda t, s: (t, s ^ 1))
    both = add_cores(keep, shift(send, lambda t, s: (t, s ^ 1)))
    rows = lax.all_to_all(both, ("y", "xh"), 0, 0, tiled=True)
    inner, kern = decode(core, mine, other, prev, features, norm_gain)
    rows, inner, prev_edges, next_edges = tie((rows, inner, prev_edges, next_edges))
    parts = lax.all_to_all(add_chips(rows), ("xl", "z0"), 0, 0, tiled=True)
    parts = lax.all_to_all(add_parts(parts, 4), "z1", 0, 0, tiled=True)
    decoded, input_grad = finish_outputs(
        kern,
        prev,
        features,
        prev_edges,
        own_edges,
        cotangent,
        edges,
        next_cot,
        next_edges,
        norm_gain,
        inner,
    )
    parts, decoded, input_grad = tie((parts, decoded, input_grad))
    whole = lax.all_to_all(add_parts(parts, 8), ("xl", "z0"), 0, 0, tiled=True)
    return (decoded, finish(whole), input_grad)


def solution(mesh):
    fine = Mesh(mesh.devices.reshape(SIZES), AXES)
    split = P(TM, SPACE, None, None)
    rows = P(SPACE, None)
    return jax.shard_map(
        on_device,
        mesh=fine,
        in_specs=(split, P(), rows, split),
        out_specs=(split, rows, split),
        check_vma=False,
    )
```

```python
import jax
import jax.numpy as jnp
from jax import lax
from jax.experimental import pallas as pl
from jax.experimental.pallas import tpu as pltpu
from jax.sharding import Mesh, PartitionSpec as P

epsilon = 1e-06
F32 = jnp.float32
BF16 = jnp.bfloat16
TM = ("xl", "z1", "z0")
SPACE = ("y", "xh", "co")
SIZES = (2, 4, 4, 4, 2, 2)
AXES = TM + SPACE
TMS, SPACES = 32, 16


def shift(block, target):
    route = []
    for t in range(TMS):
        for s in range(SPACES):
            u, v = target(t, s)
            if 0 <= u < TMS and 0 <= v < SPACES:
                route.append((t * SPACES + s, u * SPACES + v))
    return lax.ppermute(block, AXES, route)


def beside(block):
    cols = block.shape[1]
    col = lax.broadcasted_iota(jnp.int32, block.shape, 1)
    left = jnp.where(col == 0, 0.0, pltpu.roll(block, 1, 1))
    right = jnp.where(col == cols - 1, 0.0, pltpu.roll(block, cols - 1, 1))
    return jnp.concatenate([left, block, right], axis=-1).astype(BF16)


def activated(block, gain):
    frames, rows, cols, channels = block.shape
    v = block.reshape(frames * rows, cols, channels).astype(F32)
    z = v * lax.rsqrt(jnp.mean(v * v, axis=-1, keepdims=True) + epsilon) * gain
    return z / (1.0 + jnp.exp(-z))


def gradient(act, pad):
    frames = act.shape[0]
    rows = act.reshape(frames * 640, 384)
    shifted = [pad[:, 2 - b : 10 - b].reshape(frames * 640, 256) for b in range(3)]
    return lax.dot_general(
        rows,
        jnp.concatenate(shifted, axis=-1),
        (((0,), (0,)), ((), ())),
        preferred_element_type=F32,
    )


def kernel_grad_body(
    core, prev, own, gain, cot, top, low, cot_edges, row_edges, keep, send, act, pad, part, total
):
    g = gain[...].reshape(1, 1, 128)
    act[2:4] = beside(activated(own[...], g)).reshape(2, 8, 80, 384)
    act[0:2] = beside(activated(prev[...], g)).reshape(2, 8, 80, 384)
    for index, outer in enumerate((top, low)):
        row_edges[:, index : index + 1] = outer[:, :, :, :128]
        cot_edges[:, index : index + 1] = outer[:, :, :, 128:]
        pad[:, 9 * index : 9 * index + 1] = outer[:, :, :, 128:]
    pad[:, 1:9] = cot[...]
    for a in range(3):
        part_of = total.at[a] if a < 2 else part
        part_of[...] = gradient(act[a : a + 2], pad[...])

    def tap(index):
        a, b, e = index // 9, index // 3 % 3, index % 3
        ref = part if a == 2 else total.at[a]
        return ref, 128 * e, 256 * b

    def pack(even, odd):
        for pair in range(14):
            for chip in range(8):
                for out, parity in ((even, 0), (odd, 1)):
                    blocks = []
                    for index in (2 * pair, min(2 * pair + 1, 26)):
                        ref, row, col = tap(index)
                        row = row + 16 * chip + 8 * parity
                        blocks.append(ref[row : row + 8, col : col + 256])
                    if pair == 13:
                        blocks[1] = jnp.zeros_like(blocks[1])
                    both = jnp.concatenate(blocks, axis=0).astype(BF16)
                    out[chip, 16 * pair : 16 * pair + 16] = both

    @pl.when(core[0] == 0)
    def _():
        pack(keep, send)

    @pl.when(core[0] != 0)
    def _():
        pack(send, keep)


VMEM = pl.BlockSpec(memory_space=pltpu.VMEM)
SMEM = pl.BlockSpec(memory_space=pltpu.SMEM)
ANY = pl.BlockSpec(memory_space=pl.ANY)


def kernel_gradient(core, prev, own, gain, cot, top, low):
    return pl.pallas_call(
        kernel_grad_body,
        out_shape=(
            jax.ShapeDtypeStruct((2, 2, 80, 256), BF16),
            jax.ShapeDtypeStruct((2, 2, 80, 128), BF16),
            jax.ShapeDtypeStruct((8, 224, 256), BF16),
            jax.ShapeDtypeStruct((8, 224, 256), BF16),
        ),
        in_specs=[SMEM] + [VMEM] * 6,
        out_specs=(VMEM,) * 4,
        scratch_shapes=[
            pltpu.VMEM((4, 8, 80, 384), BF16),
            pltpu.VMEM((2, 10, 80, 256), BF16),
            pltpu.VMEM((384, 768), F32),
            pltpu.VMEM((2, 384, 768), F32),
        ],
        compiler_params=pltpu.CompilerParams(vmem_limit_bytes=20 << 20),
        cost_estimate=pl.CostEstimate(
            flops=2 * 1280 * 3456 * 256, bytes_accessed=6 << 20, transcendentals=1 << 18
        ),
        name="kernel_grad",
    )(core, prev, own, gain, cot, top, low)


def call(body, name, out_shape, args, specs=None, scratch=()):
    return pl.pallas_call(
        body,
        out_shape=out_shape,
        in_specs=specs or [VMEM] * len(args),
        out_specs=VMEM,
        scratch_shapes=scratch,
        compiler_params=pltpu.CompilerParams(vmem_limit_bytes=6 << 20),
        name=name,
    )(*args)


def add_cores(keep, got):
    def body(keep_ref, got_ref, out_ref):
        out_ref[...] = (keep_ref[...].astype(F32) + got_ref[...].astype(F32)).astype(BF16)

    shape = jax.ShapeDtypeStruct(keep.shape, BF16)
    return call(body, "add_cores", shape, (keep, got))


def add_chips(rows):
    def body(rows_ref, out_ref):
        total = rows_ref[0].astype(F32)
        for chip in range(1, 8):
            total = total + rows_ref[chip].astype(F32)
        for side in range(2):
            for quarter in range(4):
                block = total[56 * quarter : 56 * quarter + 56, 128 * side : 128 * side + 128]
                out_ref[4 * side + quarter] = block

    shape = jax.ShapeDtypeStruct((8, 56, 128), F32)
    return call(body, "add_chips", shape, (rows,))


def add_parts(parts, copies):
    shape = (copies, *parts.shape[1:])

    def body(parts_ref, out_ref):
        total = parts_ref[0]
        for index in range(1, parts.shape[0]):
            total = total + parts_ref[index]
        out_ref[...] = jnp.broadcast_to(total, shape)

    return call(body, "add_parts", jax.ShapeDtypeStruct(shape, F32), (parts,))


def repeat(rows, copies):
    shape = (copies, *rows.shape)

    def body(rows_ref, out_ref):
        for index in range(copies):
            out_ref[index] = rows_ref[...]

    return call(body, "repeat", jax.ShapeDtypeStruct(shape, rows.dtype), (rows,))


def finish(whole):
    def body(whole_ref, out_ref, side_ref):
        for side in range(2):
            for tap in range(27):
                row = 8 * tap
                block = whole_ref[4 * side + row // 56, row % 56 : row % 56 + 8]
                side_ref[side, pl.ds(tap, 8, stride=27), :] = block
            out_ref[:, 128 * side : 128 * side + 128] = side_ref[side]

    shape = jax.ShapeDtypeStruct((216, 256), F32)
    scratch = (pltpu.VMEM((2, 216, 128), F32),)
    return call(body, "finish", shape, (whole,), None, scratch)


def decode_body(
    core,
    mine_hbm,
    other_hbm,
    prev_hbm,
    own_hbm,
    prev_edges,
    own_edges,
    gain,
    dec_hbm,
    kern_hbm,
    kern,
    raw,
    act,
    mine,
    other,
    prev,
    own,
    dec,
    sems,
):
    pairs = ((mine_hbm, mine), (other_hbm, other), (prev_hbm, prev), (own_hbm, own))
    loads = [
        pltpu.make_async_copy(source, held, sems.at[index])
        for index, (source, held) in enumerate(pairs)
    ]
    for load in loads:
        load.start()
    loads[0].wait()
    loads[1].wait()
    for chip in range(8):
        for side in range(2):
            columns = slice(128 * side, 128 * side + 128)
            one, two = [ref[chip, :, columns].astype(F32) for ref in (mine, other)]
            raw[side, 0] = jnp.where(core[0] == 0, one, two)
            raw[side, 1] = jnp.where(core[0] == 0, two, one)
            for tap in range(27):
                rows = [raw[side, half, pl.ds(tap, 8, stride=27), :] for half in range(2)]
                rows = jnp.concatenate(rows, axis=0).astype(BF16)
                kern[tap, 16 * chip : 16 * chip + 16, columns] = rows
    stores = [pltpu.make_async_copy(kern, kern_hbm, sems.at[4])]
    stores[0].start()
    loads[2].wait()
    loads[3].wait()
    g = gain[...].reshape(1, 1, 128)
    for frame, block, outer in ((0, prev, prev_edges), (2, own, own_edges)):
        frames = slice(frame, frame + 2)
        act[frames, 1:9] = beside(activated(block[...], g)).reshape(2, 8, 80, 384)
        edge = beside(activated(outer[...], g)).reshape(2, 2, 80, 384)
        act[frames, 0:1] = edge[:, 0:1]
        act[frames, 9:10] = edge[:, 1:2]
    for t in range(2):
        for half in range(2):
            at = 4 * half
            patches = [
                act[t + a, at + b : at + b + 4].reshape(320, 384)
                for a in range(3)
                for b in range(3)
            ]
            out = jnp.dot(
                jnp.concatenate(patches, axis=-1),
                kern[...].reshape(3456, 256),
                preferred_element_type=F32,
            )
            dec[t, at : at + 4] = out.astype(BF16).reshape(4, 80, 256)
            stores.append(
                pltpu.make_async_copy(
                    dec.at[t, at : at + 4], dec_hbm.at[t, at : at + 4], sems.at[5 + 2 * t + half]
                )
            )
            stores[-1].start()
    for store in stores:
        store.wait()


def decode(core, mine, other, prev, own, prev_edges, own_edges, gain):
    return pl.pallas_call(
        decode_body,
        out_shape=(
            jax.ShapeDtypeStruct((2, 8, 80, 256), BF16),
            jax.ShapeDtypeStruct((27, 128, 256), BF16),
        ),
        in_specs=[SMEM] + [ANY] * 4 + [VMEM] * 3,
        out_specs=(ANY, ANY),
        scratch_shapes=[
            pltpu.VMEM((27, 128, 256), BF16),
            pltpu.VMEM((2, 2, 216, 128), F32),
            pltpu.VMEM((4, 10, 80, 384), BF16),
            pltpu.VMEM((8, 216, 256), BF16),
            pltpu.VMEM((8, 216, 256), BF16),
            pltpu.VMEM((2, 8, 80, 128), BF16),
            pltpu.VMEM((2, 8, 80, 128), BF16),
            pltpu.VMEM((2, 8, 80, 256), BF16),
            pltpu.SemaphoreType.DMA((9,)),
        ],
        compiler_params=pltpu.CompilerParams(vmem_limit_bytes=60 << 20),
        cost_estimate=pl.CostEstimate(
            flops=2 * 1280 * 3456 * 256, bytes_accessed=8 << 20, transcendentals=0
        ),
        name="decode",
    )(core, mine, other, prev, own, prev_edges, own_edges, gain)


def input_grad_body(
    kern_hbm,
    own_hbm,
    cot_hbm,
    edges,
    next_cot_hbm,
    next_edges,
    gain,
    ing,
    kern,
    own,
    cot,
    next_cot,
    sems,
):
    pairs = [(cot_hbm, cot), (next_cot_hbm, next_cot), (own_hbm, own)]
    for a in range(3):
        taps = slice(9 * a, 9 * a + 9)
        pairs.append((kern_hbm.at[taps], kern.at[taps]))
    loads = [
        pltpu.make_async_copy(source, held, sems.at[index])
        for index, (source, held) in enumerate(pairs)
    ]
    for index in (0, 5, 4, 1, 3, 2):
        loads[index].start()
    g = gain[...].reshape(1, 1, 128)
    loads[0].wait()

    def cot_rows(frame, at):
        ref, outer, frame = (
            (cot, edges, frame) if frame < 2 else (next_cot, next_edges, frame - 2)
        )
        if at < 0:
            rows = jnp.concatenate([outer[frame, 0:1], ref[frame, 0:3]], axis=0)
        elif at > 4:
            rows = jnp.concatenate([ref[frame, 5:8], outer[frame, 1:2]], axis=0)
        else:
            rows = ref[frame, at : at + 4]
        return rows.reshape(320, 256)

    for s in range(2):
        for half in range(2):
            sums = jnp.zeros((320, 384), F32)
            for a in (2, 1, 0):
                if s == 0 and half == 0:
                    loads[3 + a].wait()
                    if a == 0:
                        loads[1].wait()
                for b in range(3):
                    window = cot_rows(s + 2 - a, 4 * half + 1 - b)
                    weights = kern[9 * a + 3 * b : 9 * a + 3 * b + 3].reshape(384, 256)
                    sums = sums + lax.dot_general(
                        window, weights, (((1,), (1,)), ((), ())), preferred_element_type=F32
                    )
            sums = sums.reshape(4, 80, 384)
            left, mid, right = sums[..., :128], sums[..., 128:256], sums[..., 256:]
            col = lax.broadcasted_iota(jnp.int32, mid.shape, 1)
            grad = mid + jnp.where(col == 79, 0.0, pltpu.roll(left, 79, 1))
            grad = grad + jnp.where(col == 0, 0.0, pltpu.roll(right, 1, 1))
            if s == 0 and half == 0:
                loads[2].wait()
            v = own[s, 4 * half : 4 * half + 4].astype(F32)
            scale = lax.rsqrt(jnp.mean(v * v, axis=-1, keepdims=True) + epsilon)
            normed = v * scale
            z = normed * g
            gate = 1.0 / (1.0 + jnp.exp(-z))
            dn = grad * (gate * (1.0 + z * (1.0 - gate))) * g
            out = scale * (dn - normed * jnp.mean(dn * normed, axis=-1, keepdims=True))
            ing[s, 4 * half : 4 * half + 4] = out.astype(BF16)


def input_gradient(kern, own, cot, edges, next_cot, next_edges, gain):
    return pl.pallas_call(
        input_grad_body,
        out_shape=jax.ShapeDtypeStruct((2, 8, 80, 128), BF16),
        in_specs=[ANY] * 3 + [VMEM, ANY, VMEM, VMEM],
        out_specs=VMEM,
        scratch_shapes=[
            pltpu.VMEM((27, 128, 256), BF16),
            pltpu.VMEM((2, 8, 80, 128), BF16),
            pltpu.VMEM((2, 8, 80, 256), BF16),
            pltpu.VMEM((2, 8, 80, 256), BF16),
            pltpu.SemaphoreType.DMA((6,)),
        ],
        compiler_params=pltpu.CompilerParams(vmem_limit_bytes=60 << 20),
        cost_estimate=pl.CostEstimate(
            flops=2 * 1280 * 3456 * 256, bytes_accessed=8 << 20, transcendentals=1 << 18
        ),
        name="input_grad",
    )(kern, own, cot, edges, next_cot, next_edges, gain)


def on_device(features, norm_gain, kernel, cotangent):
    core = lax.axis_index("co").reshape(1)
    tie = lax.optimization_barrier
    next_cot = shift(cotangent, lambda t, s: (t - 1, s))
    prev = shift(features, lambda t, s: (t + 1, s))
    last = jnp.concatenate([features[:, 7:], cotangent[:, 7:]], axis=-1)
    first = jnp.concatenate([features[:, :1], cotangent[:, :1]], axis=-1)
    top = shift(last, lambda t, s: (t, s + 1))
    low = shift(first, lambda t, s: (t, s - 1))
    next_cot, prev, top, low, repeated = tie((next_cot, prev, top, low, repeat(kernel, 8)))
    mine = lax.all_to_all(repeated, ("y", "xh"), 0, 0, tiled=True)
    edges, own_edges, keep, send = kernel_gradient(
        core, prev, features, norm_gain, cotangent, top, low
    )
    next_edges = shift(edges, lambda t, s: (t - 1, s))
    prev_edges = shift(own_edges, lambda t, s: (t + 1, s))
    keep, mine, prev_edges = tie((keep, mine, prev_edges))
    other = shift(mine, lambda t, s: (t, s ^ 1))
    both = add_cores(keep, shift(send, lambda t, s: (t, s ^ 1)))
    rows = lax.all_to_all(both, ("y", "xh"), 0, 0, tiled=True)
    decoded, kern = decode(
        core, mine, other, prev, features, prev_edges, own_edges, norm_gain
    )
    rows, decoded, next_edges = tie((rows, decoded, next_edges))
    parts = lax.all_to_all(add_chips(rows), ("xl", "z0"), 0, 0, tiled=True)
    parts = lax.all_to_all(add_parts(parts, 4), "z1", 0, 0, tiled=True)
    input_grad = input_gradient(
        kern, features, cotangent, edges, next_cot, next_edges, norm_gain
    )
    parts, input_grad = tie((parts, input_grad))
    whole = lax.all_to_all(add_parts(parts, 8), ("xl", "z0"), 0, 0, tiled=True)
    return (decoded, finish(whole), input_grad)


def solution(mesh):
    fine = Mesh(mesh.devices.reshape(SIZES), AXES)
    split = P(TM, SPACE, None, None)
    rows = P(SPACE, None)
    return jax.shard_map(
        on_device,
        mesh=fine,
        in_specs=(split, P(), rows, split),
        out_specs=(split, rows, split),
        check_vma=False,
    )
```
